32 devices in a mesh: copies: 2 (over y), row: 4 (over z), col: 4 (over x, core).
Axes of the slice: x: 2, y: 2, z: 4, core: 2. Of those that a mesh axis runs over, the one named last changes fastest.
Arguments:
- multiple_alignment_tensor: bfloat16 [128, 128, 256], P(('copies', 'col'), 'row'), parts along dimension 0, may hold values from -1000 to 1000
- standardize_multiplier: float32 [256], replicated, may hold values from 0.1 to 1.9
- standardize_shift: float32 [256], replicated, may hold values from -3 to 3
- lhs_embedding_matrix: bfloat16 [256, 32], replicated, may hold values from -0.375 to 0.375
- lhs_embedding_shift: float32 [32], replicated, may hold values from -4 to 4
- rhs_embedding_matrix: bfloat16 [256, 32], replicated, may hold values from -0.375 to 0.375
- rhs_embedding_shift: float32 [32], replicated, may hold values from -4 to 4
- final_mapping_matrix: bfloat16 [1024, 128], replicated, may hold values from -0.1875 to 0.1875
- final_mapping_shift: float32 [128], replicated, may hold values from -3 to 3
Outputs:
- pair_update: bfloat16 [256, 128, 128], P(('copies', 'row'), 'col'), parts along dimension 0
The draws below stay inside these ranges and needn't reach their ends.
There are 2 independent parts, one for each index of `copies`. The reference program is written for one: setup_inputs(seed, part) draws one part's arguments, and reference() takes and returns one part's arrays. A program takes and returns all parts, laid end to end along the dimension named above; an argument that names none is the same for every part. Nothing has to cross between parts.
All inputs are finite; a program needn't handle non-finite values.
Results may differ from the reference program's by a relative error of at most 0.005.
Values may be sent and summed in bfloat16 or wider, within the bound.
A program may use at most 64 MiB of HBM per device.

```python
import math
import jax
import jax.numpy as jnp
from jax import lax

ALIGN_CHANNELS = 256
PROJECT_CHANNELS = 32
PAIR_CH = 128
RES_DEV = 32
SEQUENCE_COUNT = 64
RESIDUE_COUNT = 128


def draw_multiple_alignment_tensor(key, part):
    key = jax.random.fold_in(key, 11)
    first_item, second, third_item = jax.random.split(key, 3)
    rows = jnp.exp(jax.random.uniform(second, (SEQUENCE_COUNT, RESIDUE_COUNT, 1), jnp.float32) * math.log(10.0))
    channel_items = jnp.exp(jax.random.uniform(third_item, (1, 1, ALIGN_CHANNELS), jnp.float32) * math.log(10.0))
    entries_collection = jax.random.normal(first_item, (SEQUENCE_COUNT, RESIDUE_COUNT, ALIGN_CHANNELS), jnp.float32)
    entries_collection = jnp.clip(entries_collection, -5.0, 5.0)
    return (entries_collection * rows * channel_items).astype(jnp.bfloat16)


def noise(rng, shape, width, reach, kind=jnp.bfloat16):
    entries = jax.random.normal(rng, shape, jnp.float32) * width
    return jnp.minimum(jnp.maximum(entries, -reach), reach).astype(kind)


def setup_inputs(seed: int = 0, part: int = 0) -> dict:
    key_list = jax.random.split(jax.random.key(seed), 10)
    part_keys = jax.random.split(jax.random.fold_in(key_list[9], part), 10)
    multiple_alignment_tensor = draw_multiple_alignment_tensor(jax.random.fold_in(jax.random.fold_in(key_list[9], part), 71), part)
    standardize_multiplier = jnp.clip(1.0 + 0.18 * jax.random.normal(key_list[1], (ALIGN_CHANNELS,), jnp.float32), 0.1, 1.9)
    standardize_shift = noise(key_list[2], (ALIGN_CHANNELS,), 0.5, 3.0, jnp.float32)
    lhs_embedding_matrix = noise(key_list[3], (ALIGN_CHANNELS, PROJECT_CHANNELS), ALIGN_CHANNELS ** -0.5, 0.375)
    lhs_embedding_shift = noise(key_list[4], (PROJECT_CHANNELS,), 1.0, 4.0, jnp.float32)
    rhs_embedding_matrix = noise(key_list[5], (ALIGN_CHANNELS, PROJECT_CHANNELS), ALIGN_CHANNELS ** -0.5, 0.375)
    rhs_embedding_shift = noise(key_list[6], (PROJECT_CHANNELS,), 1.0, 4.0, jnp.float32)
    final_mapping_matrix = noise(key_list[7], (PROJECT_CHANNELS * PROJECT_CHANNELS, PAIR_CH), (PROJECT_CHANNELS * PROJECT_CHANNELS) ** -0.5, 0.1875)
    final_mapping_shift = noise(key_list[8], (PAIR_CH,), 0.5, 3.0, jnp.float32)
    return {"multiple_alignment_tensor": multiple_alignment_tensor, "standardize_multiplier": standardize_multiplier, "standardize_shift": standardize_shift, "lhs_embedding_matrix": lhs_embedding_matrix, "lhs_embedding_shift": lhs_embedding_shift, "rhs_embedding_matrix": rhs_embedding_matrix, "rhs_embedding_shift": rhs_embedding_shift, "final_mapping_matrix": final_mapping_matrix, "final_mapping_shift": final_mapping_shift}


def reference(multiple_alignment_tensor, standardize_multiplier, standardize_shift, lhs_embedding_matrix, lhs_embedding_shift, rhs_embedding_matrix, rhs_embedding_shift, final_mapping_matrix, final_mapping_shift):
    entries_collection = multiple_alignment_tensor.astype(jnp.float32)
    center = lax.optimization_barrier(jnp.mean(entries_collection, axis=-1, keepdims=True))
    spread = lax.optimization_barrier(jnp.mean((entries_collection - center) ** 2, axis=-1, keepdims=True))
    normed = ((entries_collection - center) * lax.rsqrt(spread + 1e-05) * standardize_multiplier + standardize_shift).astype(jnp.bfloat16)
    left = (jnp.dot(normed, lhs_embedding_matrix, preferred_element_type=jnp.float32) + lhs_embedding_shift).astype(jnp.bfloat16)
    right = (jnp.dot(normed, rhs_embedding_matrix, preferred_element_type=jnp.float32) + rhs_embedding_shift).astype(jnp.bfloat16)
    right_wide = right.astype(jnp.float32)
    blocks = RESIDUE_COUNT // RES_DEV

    def row_block(index):
        start = (index * RES_DEV).astype(jnp.int32)
        piece = lax.dynamic_slice_in_dim(left, start, RES_DEV, 1).astype(jnp.float32)
        outer = jnp.einsum('sic,sje->ijce', piece, right_wide, precision=lax.Precision.HIGHEST) / SEQUENCE_COUNT
        outer = outer.reshape(RES_DEV, RESIDUE_COUNT, PROJECT_CHANNELS * PROJECT_CHANNELS).astype(jnp.bfloat16)
        pair = jnp.dot(outer, final_mapping_matrix, preferred_element_type=jnp.float32) + final_mapping_shift
        return pair.astype(jnp.bfloat16)
    tiles = lax.map(row_block, jnp.arange(blocks, dtype=jnp.int32))
    return tiles.reshape(RESIDUE_COUNT, RESIDUE_COUNT, PAIR_CH)
```

```python
import functools

import jax
import jax.numpy as jnp
from jax import lax
from jax.experimental import pallas as pl
from jax.experimental.pallas import tpu as pltpu
from jax.sharding import PartitionSpec as P

MESH = pl.DeviceIdType.MESH
LANES = 128
F32 = jnp.float32
BF16 = jnp.bfloat16


def each(count, body):
    if count <= 4:
        for index in range(count):
            body(index)
    else:
        lax.fori_loop(0, count, lambda index, carry: (body(index), carry)[1], 0)


def kernel(
    rows,
    cols,
    x_hbm,
    gain,
    bias,
    wl,
    bl,
    wr,
    br,
    w_hbm,
    bf,
    out,
    x_v,
    w_v,
    pl_v,
    pr_v,
    l_all,
    r_all,
    r_own,
    rt_v,
    wf_v,
    we_v,
    a_v,
    x_sem,
    w_sem,
    l_send,
    l_recv,
    r_send,
    r_recv,
):
    seqs, res, channels = x_v.shape
    hidden = wl.shape[1]
    groups = LANES // hidden
    tiles = res // groups
    ratio = rows // cols
    total = seqs * cols
    outs = bf.shape[1]
    copies_at = lax.axis_index("copies")
    row = lax.axis_index("row")
    col = lax.axis_index("col")
    target = row // ratio
    stays = col == target
    own = pl.ds(pl.multiple_of(col * seqs, seqs), seqs)

    x_copy = pltpu.make_async_copy(x_hbm, x_v, x_sem)
    x_copy.start()
    w_copy = pltpu.make_async_copy(w_hbm, w_v, w_sem)
    w_copy.start()

    barrier = pltpu.get_barrier_semaphore()

    def greet_left(step):
        peer = lax.rem(col + 1 + step, cols)
        pl.semaphore_signal(barrier, 1, device_id=(copies_at, row, peer), device_id_type=MESH)

    each(cols - 1, greet_left)

    def greet_right(step):
        source_row = col * ratio + step // cols
        source_col = lax.rem(step, cols)

        @pl.when(jnp.logical_not((source_row == row) & (source_col == col)))
        def _():
            pl.semaphore_signal(
                barrier, 1, device_id=(copies_at, source_row, source_col), device_id_type=MESH
            )

    each(ratio * cols, greet_right)

    w8 = jnp.concatenate([wl[...].astype(F32)] * groups + [wr[...].astype(F32)] * groups, axis=1).astype(BF16)
    bl4 = jnp.concatenate([bl[...]] * groups, axis=1)
    br4 = jnp.concatenate([br[...]] * groups, axis=1)
    block = lax.broadcasted_iota(jnp.int32, (seqs, LANES), 1) // hidden

    x_copy.wait()
    x = x_v[...].astype(F32).reshape(seqs * res, channels)
    center = jnp.mean(x, axis=-1, keepdims=True)
    moved = x - center
    spread = jnp.mean(moved * moved, axis=-1, keepdims=True)
    normed = (moved * lax.rsqrt(spread + 1e-05) * gain[...] + bias[...]).astype(BF16)
    projected = jnp.dot(normed, w8, preferred_element_type=F32)
    pl_v[...] = projected[:, :LANES]
    pr_v[...] = projected[:, LANES:]

    def spread_out(source, shift, tile):
        value = source[pl.ds(tile * groups, seqs, stride=res), :]
        for g in range(1, groups):
            value = jnp.where(block == g, source[pl.ds(tile * groups + g, seqs, stride=res), :], value)
        return (value + shift).astype(BF16)

    for tile in range(tiles):
        r_own[:, tile * LANES : (tile + 1) * LANES] = spread_out(pr_v, br4, tile)

    @pl.when(stays)
    def _():
        r_all[lax.rem(row, ratio), own, :] = r_own[...]

    pl.semaphore_wait(barrier, cols - 1 + rows - stays.astype(jnp.int32))

    def right_copy(step):
        return pltpu.make_async_remote_copy(
            src_ref=r_own,
            dst_ref=r_all.at[lax.rem(row, ratio), own],
            send_sem=r_send.at[step],
            recv_sem=r_recv.at[lax.rem(row, ratio), col],
            device_id=(copies_at, lax.rem(row + 1 + step, rows), target),
            device_id_type=MESH,
        )

    each(rows - 1, lambda step: right_copy(step).start())

    @pl.when(jnp.logical_not(stays))
    def _():
        right_copy(rows - 1).start()

    for tile in range(tiles):
        l_all[own, tile * LANES : (tile + 1) * LANES] = spread_out(pl_v, bl4, tile)

    def left_copy(step):
        return pltpu.make_async_remote_copy(
            src_ref=l_all.at[own],
            dst_ref=l_all.at[own],
            send_sem=l_send.at[step],
            recv_sem=l_recv.at[col],
            device_id=(copies_at, row, lax.rem(col + 1 + step, cols)),
            device_id_type=MESH,
        )

    each(cols - 1, lambda step: left_copy(step).start())

    w_copy.wait()
    wf_v[...] = w_v[...].astype(F32)
    for e in range(hidden):
        we_v[e * hidden : (e + 1) * hidden, :] = wf_v[pl.ds(e, hidden, stride=hidden), :].astype(BF16)

    def left_wait(step):
        peer = lax.rem(col + 1 + step, cols)
        rows_of = pl.ds(pl.multiple_of(peer * seqs, seqs), seqs)
        pltpu.make_async_remote_copy(
            src_ref=l_all.at[rows_of],
            dst_ref=l_all.at[rows_of],
            send_sem=l_send.at[step],
            recv_sem=l_recv.at[peer],
            device_id=(copies_at, row, peer),
            device_id_type=MESH,
        ).wait_recv()

    lane_block = lax.broadcasted_iota(jnp.int32, (hidden * res // groups, 2 * LANES), 1) // hidden
    low = lax.rem(lane_block, groups) < groups // 2
    even = lax.rem(lane_block, 2) == 0

    each(cols - 1, left_wait)

    def columns(index):
        def right_wait(peer):
            rows_of = pl.ds(peer * seqs, seqs)

            @pl.when(jnp.logical_not((col * ratio + index == row) & (col == peer)))
            def _():
                pltpu.make_async_remote_copy(
                    src_ref=r_own,
                    dst_ref=r_all.at[index, rows_of],
                    send_sem=r_send.at[0],
                    recv_sem=r_recv.at[index, peer],
                    device_id=(copies_at, row, col),
                    device_id_type=MESH,
                ).wait_recv()

        for peer in range(cols):
            right_wait(peer)
        for tile in range(tiles):
            piece = r_all[index, :, tile * LANES : (tile + 1) * LANES].astype(F32)
            rt_v[tile * LANES : (tile + 1) * LANES, :total] = piece.T
        lhs = []
        for low_e in range(groups):
            parts = [
                rt_v[pl.ds(high * groups + low_e, res, stride=hidden), :].astype(BF16)
                for high in range(hidden // groups)
            ]
            lhs.append(jnp.concatenate(parts, axis=0)[:, :total])
        for pair in range(tiles // 2):
            outer = []
            for low_e in range(groups):
                rhs = []
                for tile in (2 * pair, 2 * pair + 1):
                    piece = l_all[:, tile * LANES : (tile + 1) * LANES]
                    if low_e:
                        piece = pltpu.roll(piece.astype(F32), low_e * hidden, 1).astype(BF16)
                    rhs.append(piece)
                rhs = jnp.concatenate(rhs, axis=1)
                outer.append(jnp.dot(lhs[low_e], rhs, preferred_element_type=F32).astype(BF16))
            half = [jnp.where(low, outer[-k % 4], outer[(2 - k) % 4]) for k in range(groups)]
            for low_i in range(groups):
                mixed = jnp.where(even, half[low_i], half[low_i - 1])
                for t in range(2):
                    tile = 2 * pair + t
                    for high in range(hidden // groups):
                        a_v[low_i, tile * res : (tile + 1) * res, high * LANES : (high + 1) * LANES] = mixed[
                            high * res : (high + 1) * res, t * LANES : (t + 1) * LANES
                        ]
        for low_i in range(groups):
            weights = jnp.concatenate(
                [
                    we_v[e * hidden : (e + 1) * hidden, :]
                    for high in range(hidden // groups)
                    for e in [high * groups + (b - low_i) % groups for b in range(groups)]
                ],
                axis=0,
            )
            result = jnp.dot(a_v[low_i], weights, preferred_element_type=F32)
            result = (result * (1.0 / total) + bf[...]).astype(BF16)
            for tile in range(tiles):
                at = pl.ds(pl.multiple_of(index * res, res), res)
                out[tile * groups + low_i, at, :] = result[tile * res : (tile + 1) * res, :]

    each(ratio, columns)

    each(rows - 1, lambda step: right_copy(step).wait_send())

    @pl.when(jnp.logical_not(stays))
    def _():
        right_copy(rows - 1).wait_send()

    each(cols - 1, lambda step: left_copy(step).wait_send())


def solution(mesh):
    rows, cols = mesh.shape["row"], mesh.shape["col"]

    def on_device(x, gain, bias, wl, bl, wr, br, w, bf):
        seqs, res, channels = x.shape
        hidden = wl.shape[1]
        outs = w.shape[1]
        ratio = rows // cols
        total = seqs * cols
        wide = res * hidden
        vmem = pl.BlockSpec(memory_space=pltpu.VMEM)
        hbm = pl.BlockSpec(memory_space=pl.ANY)
        groups = LANES // hidden
        return pl.pallas_call(
            functools.partial(kernel, rows, cols),
            out_shape=jax.ShapeDtypeStruct((res, ratio * res, outs), BF16),
            in_specs=[hbm] + [vmem] * 6 + [hbm, vmem],
            out_specs=vmem,
            scratch_shapes=[
                pltpu.VMEM((seqs, res, channels), BF16),
                pltpu.VMEM(w.shape, BF16),
                pltpu.VMEM((seqs * res, LANES), F32),
                pltpu.VMEM((seqs * res, LANES), F32),
                pltpu.VMEM((total, wide), BF16),
                pltpu.VMEM((ratio, total, wide), BF16),
                pltpu.VMEM((seqs, wide), BF16),
                pltpu.VMEM((wide, LANES), F32),
                pltpu.VMEM(w.shape, F32),
                pltpu.VMEM(w.shape, BF16),
                pltpu.VMEM((groups, wide // groups, hidden * hidden), BF16),
                pltpu.SemaphoreType.DMA,
                pltpu.SemaphoreType.DMA,
                pltpu.SemaphoreType.DMA((cols - 1,)),
                pltpu.SemaphoreType.DMA((cols,)),
                pltpu.SemaphoreType.DMA((rows,)),
                pltpu.SemaphoreType.DMA((ratio, cols)),
            ],
            compiler_params=pltpu.CompilerParams(
                collective_id=0, has_side_effects=True, vmem_limit_bytes=48 * 1024 * 1024
            ),
        )(x, gain[None], bias[None], wl, bl[None], wr, br[None], w, bf[None])

    placed = (P(("copies", "col"), "row", None), P(), P(), P(), P(), P(), P(), P(), P())
    return jax.shard_map(
        on_device,
        mesh=mesh,
        in_specs=placed,
        out_specs=P(("copies", "row"), "col", None),
        check_vma=False,
    )
```

```python
import functools

import jax
import jax.numpy as jnp
from jax import lax
from jax.experimental import pallas as pl
from jax.experimental.pallas import tpu as pltpu
from jax.sharding import PartitionSpec as P

MESH = pl.DeviceIdType.MESH
LANES = 128
F32 = jnp.float32
BF16 = jnp.bfloat16


def each(count, body):
    if count <= 4:
        for index in range(count):
            body(index)
    else:
        lax.fori_loop(0, count, lambda index, carry: (body(index), carry)[1], 0)


def kernel(
    rows,
    cols,
    x_hbm,
    gain_hbm,
    bias_hbm,
    wl_hbm,
    bl_hbm,
    wr_hbm,
    br_hbm,
    w_hbm,
    bf_hbm,
    out,
    x_v,
    gain,
    bias,
    wlr,
    blr,
    w_v,
    bf,
    pl_v,
    pr_v,
    l_all,
    r_all,
    r_own,
    rt_v,
    wf_v,
    we_v,
    a_v,
    in_sem,
    l_send,
    l_recv,
    r_send,
    r_recv,
):
    seqs, res, channels = x_v.shape
    hidden = wlr.shape[0] // 2
    groups = LANES // hidden
    tiles = res // groups
    ratio = rows // cols
    total = seqs * cols
    copies_at = lax.axis_index("copies")
    row = lax.axis_index("row")
    col = lax.axis_index("col")
    target = row // ratio
    stays = col == target
    own = pl.ds(pl.multiple_of(col * seqs, seqs), seqs)

    loads = [
        pltpu.make_async_copy(source, place, in_sem.at[index])
        for index, (source, place) in enumerate(
            [
                (x_hbm, x_v),
                (wl_hbm, wlr.at[0:hidden]),
                (wr_hbm, wlr.at[hidden : 2 * hidden]),
                (gain_hbm, gain),
                (bias_hbm, bias),
                (bl_hbm, blr.at[0:1]),
                (br_hbm, blr.at[1:2]),
                (w_hbm, w_v),
                (bf_hbm, bf),
            ]
        )
    ]
    for load in loads:
        load.start()

    barrier = pltpu.get_barrier_semaphore()

    def greet_left(step):
        peer = lax.rem(col + 1 + step, cols)
        pl.semaphore_signal(barrier, 1, device_id=(copies_at, row, peer), device_id_type=MESH)

    each(cols - 1, greet_left)

    def greet_right(step):
        source_row = col * ratio + step // cols
        source_col = lax.rem(step, cols)

        @pl.when(jnp.logical_not((source_row == row) & (source_col == col)))
        def _():
            pl.semaphore_signal(
                barrier, 1, device_id=(copies_at, source_row, source_col), device_id_type=MESH
            )

    each(ratio * cols, greet_right)

    block = lax.broadcasted_iota(jnp.int32, (seqs, LANES), 1) // hidden

    for load in loads[1:7]:
        load.wait()
    left_w, right_w = wlr[:hidden, :], wlr[hidden:, :]
    w8 = jnp.concatenate([left_w] * groups + [right_w] * groups, axis=0)
    bl4 = jnp.concatenate([blr[0:1, :]] * groups, axis=1)
    br4 = jnp.concatenate([blr[1:2, :]] * groups, axis=1)
    loads[0].wait()
    x = x_v[...].astype(F32).reshape(seqs * res, channels)
    center = jnp.mean(x, axis=-1, keepdims=True)
    moved = x - center
    spread = jnp.mean(moved * moved, axis=-1, keepdims=True)
    normed = (moved * lax.rsqrt(spread + 1e-05) * gain[...] + bias[...]).astype(BF16)
    projected = lax.dot_general(normed, w8, (((1,), (1,)), ((), ())), preferred_element_type=F32)
    pl_v[...] = projected[:, :LANES]
    pr_v[...] = projected[:, LANES:]

    def spread_out(source, shift, tile):
        value = source[pl.ds(tile * groups, seqs, stride=res), :]
        for g in range(1, groups):
            value = jnp.where(block == g, source[pl.ds(tile * groups + g, seqs, stride=res), :], value)
        return (value + shift).astype(BF16)

    for tile in range(tiles):
        r_own[:, tile * LANES : (tile + 1) * LANES] = spread_out(pr_v, br4, tile)

    @pl.when(stays)
    def _():
        r_all[lax.rem(row, ratio), own, :] = r_own[...]

    pl.semaphore_wait(barrier, cols - 1 + rows - stays.astype(jnp.int32))

    def right_copy(step):
        return pltpu.make_async_remote_copy(
            src_ref=r_own,
            dst_ref=r_all.at[lax.rem(row, ratio), own],
            send_sem=r_send.at[step],
            recv_sem=r_recv.at[lax.rem(row, ratio), col],
            device_id=(copies_at, lax.rem(row + 1 + step, rows), target),
            device_id_type=MESH,
        )

    each(rows - 1, lambda step: right_copy(step).start())

    @pl.when(jnp.logical_not(stays))
    def _():
        right_copy(rows - 1).start()

    for tile in range(tiles):
        l_all[own, tile * LANES : (tile + 1) * LANES] = spread_out(pl_v, bl4, tile)

    def left_copy(step):
        return pltpu.make_async_remote_copy(
            src_ref=l_all.at[own],
            dst_ref=l_all.at[own],
            send_sem=l_send.at[step],
            recv_sem=l_recv.at[col],
            device_id=(copies_at, row, lax.rem(col + 1 + step, cols)),
            device_id_type=MESH,
        )

    each(cols - 1, lambda step: left_copy(step).start())

    loads[7].wait()
    loads[8].wait()
    wf_v[...] = w_v[...].astype(F32)
    for e in range(hidden):
        we_v[e * hidden : (e + 1) * hidden, :] = wf_v[pl.ds(e, hidden, stride=hidden), :].astype(BF16)

    def left_wait(step):
        peer = lax.rem(col + 1 + step, cols)
        rows_of = pl.ds(pl.multiple_of(peer * seqs, seqs), seqs)
        pltpu.make_async_remote_copy(
            src_ref=l_all.at[rows_of],
            dst_ref=l_all.at[rows_of],
            send_sem=l_send.at[step],
            recv_sem=l_recv.at[peer],
            device_id=(copies_at, row, peer),
            device_id_type=MESH,
        ).wait_recv()

    lane_block = lax.broadcasted_iota(jnp.int32, (hidden * res // groups, 2 * LANES), 1) // hidden
    low = lax.rem(lane_block, groups) < groups // 2
    even = lax.rem(lane_block, 2) == 0

    each(cols - 1, left_wait)

    def columns(index):
        def right_wait(peer):
            rows_of = pl.ds(peer * seqs, seqs)

            @pl.when(jnp.logical_not((col * ratio + index == row) & (col == peer)))
            def _():
                pltpu.make_async_remote_copy(
                    src_ref=r_own,
                    dst_ref=r_all.at[index, rows_of],
                    send_sem=r_send.at[0],
                    recv_sem=r_recv.at[index, peer],
                    device_id=(copies_at, row, col),
                    device_id_type=MESH,
                ).wait_recv()

        for peer in range(cols):
            right_wait(peer)
        for tile in range(tiles):
            piece = r_all[index, :, tile * LANES : (tile + 1) * LANES].astype(F32)
            rt_v[tile * LANES : (tile + 1) * LANES, :total] = piece.T
        lhs = []
        for low_e in range(groups):
            parts = [
                rt_v[pl.ds(high * groups + low_e, res, stride=hidden), :].astype(BF16)
                for high in range(hidden // groups)
            ]
            lhs.append(jnp.concatenate(parts, axis=0)[:, :total])
        for pair in range(tiles // 2):
            outer = []
            for low_e in range(groups):
                rhs = []
                for tile in (2 * pair, 2 * pair + 1):
                    piece = l_all[:, tile * LANES : (tile + 1) * LANES]
                    if low_e:
                        piece = pltpu.roll(piece.astype(F32), low_e * hidden, 1).astype(BF16)
                    rhs.append(piece)
                rhs = jnp.concatenate(rhs, axis=1)
                outer.append(jnp.dot(lhs[low_e], rhs, preferred_element_type=F32).astype(BF16))
            half = [jnp.where(low, outer[-k % 4], outer[(2 - k) % 4]) for k in range(groups)]
            for low_i in range(groups):
                mixed = jnp.where(even, half[low_i], half[low_i - 1])
                for t in range(2):
                    tile = 2 * pair + t
                    for high in range(hidden // groups):
                        a_v[low_i, tile * res : (tile + 1) * res, high * LANES : (high + 1) * LANES] = mixed[
                            high * res : (high + 1) * res, t * LANES : (t + 1) * LANES
                        ]
        for low_i in range(groups):
            weights = jnp.concatenate(
                [
                    we_v[e * hidden : (e + 1) * hidden, :]
                    for high in range(hidden // groups)
                    for e in [high * groups + (b - low_i) % groups for b in range(groups)]
                ],
                axis=0,
            )
            result = jnp.dot(a_v[low_i], weights, preferred_element_type=F32)
            result = (result * (1.0 / total) + bf[...]).astype(BF16)
            for tile in range(tiles):
                at = pl.ds(pl.multiple_of(index * res, res), res)
                out[tile * groups + low_i, at, :] = result[tile * res : (tile + 1) * res, :]

    each(ratio, columns)

    each(rows - 1, lambda step: right_copy(step).wait_send())

    @pl.when(jnp.logical_not(stays))
    def _():
        right_copy(rows - 1).wait_send()

    each(cols - 1, lambda step: left_copy(step).wait_send())


def solution(mesh):
    rows, cols = mesh.shape["row"], mesh.shape["col"]

    def on_device(x, gain, bias, wl, bl, wr, br, w, bf):
        seqs, res, channels = x.shape
        hidden = wl.shape[1]
        outs = w.shape[1]
        ratio = rows // cols
        total = seqs * cols
        wide = res * hidden
        vmem = pl.BlockSpec(memory_space=pltpu.VMEM)
        hbm = pl.BlockSpec(memory_space=pltpu.HBM)
        groups = LANES // hidden
        return pl.pallas_call(
            functools.partial(kernel, rows, cols),
            out_shape=pltpu.VMEM((res, ratio * res, outs), BF16),
            in_specs=[hbm] * 9,
            out_specs=vmem,
            scratch_shapes=[
                pltpu.VMEM((seqs, res, channels), BF16),
                pltpu.VMEM((1, channels), F32),
                pltpu.VMEM((1, channels), F32),
                pltpu.VMEM((2 * hidden, channels), BF16),
                pltpu.VMEM((2, hidden), F32),
                pltpu.VMEM(w.shape, BF16),
                pltpu.VMEM((1, outs), F32),
                pltpu.VMEM((seqs * res, LANES), F32),
                pltpu.VMEM((seqs * res, LANES), F32),
                pltpu.VMEM((total, wide), BF16),
                pltpu.VMEM((ratio, total, wide), BF16),
                pltpu.VMEM((seqs, wide), BF16),
                pltpu.VMEM((wide, LANES), F32),
                pltpu.VMEM(w.shape, F32),
                pltpu.VMEM(w.shape, BF16),
                pltpu.VMEM((groups, wide // groups, hidden * hidden), BF16),
                pltpu.SemaphoreType.DMA((9,)),
                pltpu.SemaphoreType.DMA((cols - 1,)),
                pltpu.SemaphoreType.DMA((cols,)),
                pltpu.SemaphoreType.DMA((rows,)),
                pltpu.SemaphoreType.DMA((ratio, cols)),
            ],
            compiler_params=pltpu.CompilerParams(
                collective_id=0, has_side_effects=True, vmem_limit_bytes=48 * 1024 * 1024
            ),
        )(*[pltpu.with_memory_space_constraint(v, pltpu.HBM) for v in (x, gain[None], bias[None], wl.T, bl[None], wr.T, br[None], w, bf[None])])

    placed = (P(("copies", "col"), "row", None), P(), P(), P(), P(), P(), P(), P(), P())
    return jax.shard_map(
        on_device,
        mesh=mesh,
        in_specs=placed,
        out_specs=P(("copies", "row"), "col", None),
        check_vma=False,
    )
```

```python
import functools

import jax
import jax.numpy as jnp
from jax import lax
from jax.experimental import pallas as pl
from jax.experimental.pallas import tpu as pltpu
from jax.sharding import PartitionSpec as P

MESH = pl.DeviceIdType.MESH
LANES = 128
X_PARTS = 1
F32 = jnp.float32
BF16 = jnp.bfloat16


def each(count, body):
    if count <= 4:
        for index in range(count):
            body(index)
    else:
        lax.fori_loop(0, count, lambda index, carry: (body(index), carry)[1], 0)


def kernel(
    rows,
    cols,
    x_hbm,
    gain_hbm,
    bias_hbm,
    wl_hbm,
    bl_hbm,
    wr_hbm,
    br_hbm,
    w_hbm,
    bf_hbm,
    out,
    x_v,
    gain,
    bias,
    wlr,
    blr,
    w_v,
    bf,
    pl_v,
    pr_v,
    l_all,
    r_all,
    r_own,
    rt_v,
    wf_v,
    we_v,
    rolled_v,
    a_v,
    x_sem,
    in_sem,
    l_send,
    l_recv,
    r_send,
    r_recv,
):
    seqs, res, channels = x_v.shape
    hidden = wlr.shape[0] // 2
    groups = LANES // hidden
    tiles = res // groups
    ratio = rows // cols
    total = seqs * cols
    copies_at = lax.axis_index("copies")
    row = lax.axis_index("row")
    col = lax.axis_index("col")
    target = row // ratio
    stays = col == target
    own = pl.ds(pl.multiple_of(col * seqs, seqs), seqs)

    barrier = pltpu.get_barrier_semaphore()

    def greet_left(step):
        peer = lax.rem(col + 1 + step, cols)
        pl.semaphore_signal(barrier, 1, device_id=(copies_at, row, peer), device_id_type=MESH)

    each(cols - 1, greet_left)

    def greet_right(step):
        source_row = col * ratio + step // cols
        source_col = lax.rem(step, cols)

        @pl.when(jnp.logical_not((source_row == row) & (source_col == col)))
        def _():
            pl.semaphore_signal(
                barrier, 1, device_id=(copies_at, source_row, source_col), device_id_type=MESH
            )

    each(ratio * cols, greet_right)

    loads = [
        pltpu.make_async_copy(source, place, in_sem.at[index])
        for index, (source, place) in enumerate(
            [
                (wl_hbm, wlr.at[0:hidden]),
                (wr_hbm, wlr.at[hidden : 2 * hidden]),
                (gain_hbm, gain),
                (bias_hbm, bias),
                (bl_hbm, blr.at[0:1]),
                (br_hbm, blr.at[1:2]),
                (w_hbm, w_v),
                (bf_hbm, bf),
            ]
        )
    ]
    x_part = seqs // X_PARTS
    x_loads = [
        pltpu.make_async_copy(
            x_hbm.at[part * x_part : (part + 1) * x_part],
            x_v.at[part * x_part : (part + 1) * x_part],
            x_sem.at[part],
        )
        for part in range(X_PARTS)
    ]
    for load in x_loads + loads[:6]:
        load.start()

    block = lax.broadcasted_iota(jnp.int32, (seqs, LANES), 1) // hidden

    for load in loads[:6]:
        load.wait()
    left_w, right_w = wlr[:hidden, :], wlr[hidden:, :]
    w8 = jnp.concatenate([left_w] * groups + [right_w] * groups, axis=0)
    bl4 = jnp.concatenate([blr[0:1, :]] * groups, axis=1)
    br4 = jnp.concatenate([blr[1:2, :]] * groups, axis=1)
    for part in range(X_PARTS):
        x_loads[part].wait()
        if part == X_PARTS - 1:
            loads[6].start()
            loads[7].start()
        x = x_v[part * x_part : (part + 1) * x_part].astype(F32).reshape(x_part * res, channels)
        center = jnp.mean(x, axis=-1, keepdims=True)
        moved = x - center
        spread = jnp.mean(moved * moved, axis=-1, keepdims=True)
        normed = (moved * lax.rsqrt(spread + 1e-05) * gain[...] + bias[...]).astype(BF16)
        projected = lax.dot_general(normed, w8, (((1,), (1,)), ((), ())), preferred_element_type=F32)
        at = slice(part * x_part * res, (part + 1) * x_part * res)
        pl_v[at, :] = projected[:, :LANES]
        pr_v[at, :] = projected[:, LANES:]

    def spread_out(source, shift, tile):
        value = source[pl.ds(tile * groups, seqs, stride=res), :]
        for g in range(1, groups):
            value = jnp.where(block == g, source[pl.ds(tile * groups + g, seqs, stride=res), :], value)
        return (value + shift).astype(BF16)

    for tile in range(tiles):
        r_own[:, tile * LANES : (tile + 1) * LANES] = spread_out(pr_v, br4, tile)

    @pl.when(stays)
    def _():
        r_all[lax.rem(row, ratio), own, :] = r_own[...]

    for tile in range(tiles):
        l_all[own, tile * LANES : (tile + 1) * LANES] = spread_out(pl_v, bl4, tile)

    pl.semaphore_wait(barrier, cols - 1 + rows - stays.astype(jnp.int32))

    def right_copy(step):
        return pltpu.make_async_remote_copy(
            src_ref=r_own,
            dst_ref=r_all.at[lax.rem(row, ratio), own],
            send_sem=r_send.at[step],
            recv_sem=r_recv.at[lax.rem(row, ratio), col],
            device_id=(copies_at, lax.rem(row + 1 + step, rows), target),
            device_id_type=MESH,
        )

    each(rows - 1, lambda step: right_copy(step).start())

    @pl.when(jnp.logical_not(stays))
    def _():
        right_copy(rows - 1).start()

    def left_copy(step):
        return pltpu.make_async_remote_copy(
            src_ref=l_all.at[own],
            dst_ref=l_all.at[own],
            send_sem=l_send.at[step],
            recv_sem=l_recv.at[col],
            device_id=(copies_at, row, lax.rem(col + 1 + step, cols)),
            device_id_type=MESH,
        )

    each(cols - 1, lambda step: left_copy(step).start())

    loads[6].wait()
    loads[7].wait()
    wf_v[...] = w_v[...].astype(F32)
    for e in range(hidden):
        we_v[e * hidden : (e + 1) * hidden, :] = wf_v[pl.ds(e, hidden, stride=hidden), :].astype(BF16)

    def left_wait(step):
        peer = lax.rem(col + 1 + step, cols)
        rows_of = pl.ds(pl.multiple_of(peer * seqs, seqs), seqs)
        pltpu.make_async_remote_copy(
            src_ref=l_all.at[rows_of],
            dst_ref=l_all.at[rows_of],
            send_sem=l_send.at[step],
            recv_sem=l_recv.at[peer],
            device_id=(copies_at, row, peer),
            device_id_type=MESH,
        ).wait_recv()

    lane_block = lax.rem(lax.broadcasted_iota(jnp.int32, (total, 2 * LANES), 1) // hidden, groups)

    each(cols - 1, left_wait)
    for tile in range(tiles):
        lanes = slice(tile * LANES, (tile + 1) * LANES)
        piece = l_all[:, lanes]
        rolled_v[0, :, lanes] = piece
        for low_e in range(1, groups):
            rolled_v[low_e, :, lanes] = pltpu.roll(piece.astype(F32), low_e * hidden, 1).astype(BF16)

    def columns(index):
        def right_wait(peer):
            rows_of = pl.ds(peer * seqs, seqs)

            @pl.when(jnp.logical_not((col * ratio + index == row) & (col == peer)))
            def _():
                pltpu.make_async_remote_copy(
                    src_ref=r_own,
                    dst_ref=r_all.at[index, rows_of],
                    send_sem=r_send.at[0],
                    recv_sem=r_recv.at[index, peer],
                    device_id=(copies_at, row, col),
                    device_id_type=MESH,
                ).wait_recv()

        for peer in range(cols):
            right_wait(peer)
        for tile in range(tiles):
            piece = r_all[index, :, tile * LANES : (tile + 1) * LANES].astype(F32)
            rt_v[tile * LANES : (tile + 1) * LANES, :total] = piece.T
        highs = hidden // groups
        lhs = jnp.concatenate(
            [
                jnp.concatenate(
                    [
                        rt_v[pl.ds(high * groups + low_e, res, stride=hidden), :][:, :total]
                        for low_e in range(groups)
                    ],
                    axis=1,
                ).astype(BF16)
                for high in range(highs)
            ],
            axis=0,
        )
        for low_i in range(groups):
            for pair in range(tiles // 2):
                lanes = slice(2 * pair * LANES, 2 * (pair + 1) * LANES)
                rhs = jnp.concatenate(
                    [
                        jnp.where(lane_block == (low_e + low_i) % groups, rolled_v[low_e, :, lanes], 0)
                        for low_e in range(groups)
                    ],
                    axis=0,
                )
                outer = jnp.dot(lhs, rhs, preferred_element_type=F32).astype(BF16)
                for t in range(2):
                    tile = 2 * pair + t
                    for high in range(highs):
                        a_v[low_i, tile * res : (tile + 1) * res, high * LANES : (high + 1) * LANES] = outer[
                            high * res : (high + 1) * res, t * LANES : (t + 1) * LANES
                        ]
        for low_i in range(groups):
            weights = jnp.concatenate(
                [
                    we_v[e * hidden : (e + 1) * hidden, :]
                    for high in range(hidden // groups)
                    for e in [high * groups + (b - low_i) % groups for b in range(groups)]
                ],
                axis=0,
            )
            result = jnp.dot(a_v[low_i], weights, preferred_element_type=F32)
            result = (result * (1.0 / total) + bf[...]).astype(BF16)
            for tile in range(tiles):
                at = pl.ds(pl.multiple_of(index * res, res), res)
                out[tile * groups + low_i, at, :] = result[tile * res : (tile + 1) * res, :]

    each(ratio, columns)

    each(rows - 1, lambda step: right_copy(step).wait_send())

    @pl.when(jnp.logical_not(stays))
    def _():
        right_copy(rows - 1).wait_send()

    each(cols - 1, lambda step: left_copy(step).wait_send())


def solution(mesh):
    rows, cols = mesh.shape["row"], mesh.shape["col"]

    def on_device(x, gain, bias, wl, bl, wr, br, w, bf):
        seqs, res, channels = x.shape
        hidden = wl.shape[1]
        outs = w.shape[1]
        ratio = rows // cols
        total = seqs * cols
        wide = res * hidden
        vmem = pl.BlockSpec(memory_space=pltpu.VMEM)
        hbm = pl.BlockSpec(memory_space=pltpu.HBM)
        groups = LANES // hidden
        return pl.pallas_call(
            functools.partial(kernel, rows, cols),
            out_shape=pltpu.VMEM((res, ratio * res, outs), BF16),
            in_specs=[hbm] * 9,
            out_specs=vmem,
            scratch_shapes=[
                pltpu.VMEM((seqs, res, channels), BF16),
                pltpu.VMEM((1, channels), F32),
                pltpu.VMEM((1, channels), F32),
                pltpu.VMEM((2 * hidden, channels), BF16),
                pltpu.VMEM((2, hidden), F32),
                pltpu.VMEM(w.shape, BF16),
                pltpu.VMEM((1, outs), F32),
                pltpu.VMEM((seqs * res, LANES), F32),
                pltpu.VMEM((seqs * res, LANES), F32),
                pltpu.VMEM((total, wide), BF16),
                pltpu.VMEM((ratio, total, wide), BF16),
                pltpu.VMEM((seqs, wide), BF16),
                pltpu.VMEM((wide, LANES), F32),
                pltpu.VMEM(w.shape, F32),
                pltpu.VMEM(w.shape, BF16),
                pltpu.VMEM((groups, total, wide), BF16),
                pltpu.VMEM((groups, wide // groups, hidden * hidden), BF16),
                pltpu.SemaphoreType.DMA((X_PARTS,)),
                pltpu.SemaphoreType.DMA((8,)),
                pltpu.SemaphoreType.DMA((cols - 1,)),
                pltpu.SemaphoreType.DMA((cols,)),
                pltpu.SemaphoreType.DMA((rows,)),
                pltpu.SemaphoreType.DMA((ratio, cols)),
            ],
            compiler_params=pltpu.CompilerParams(
                collective_id=0, has_side_effects=True, vmem_limit_bytes=48 * 1024 * 1024
            ),
        )(*[pltpu.with_memory_space_constraint(v, pltpu.HBM) for v in (x, gain[None], bias[None], wl.T, bl[None], wr.T, br[None], w, bf[None])])

    placed = (P(("copies", "col"), "row", None), P(), P(), P(), P(), P(), P(), P(), P())
    return jax.shard_map(
        on_device,
        mesh=mesh,
        in_specs=placed,
        out_specs=P(("copies", "row"), "col", None),
        check_vma=False,
    )
```

```python
import functools

import jax
import jax.numpy as jnp
from jax import lax
from jax.experimental import pallas as pl
from jax.experimental.pallas import tpu as pltpu
from jax.sharding import PartitionSpec as P

MESH = pl.DeviceIdType.MESH
LANES = 128
X_PARTS = 1
F32 = jnp.float32
BF16 = jnp.bfloat16


def each(count, body):
    if count <= 4:
        for index in range(count):
            body(index)
    else:
        lax.fori_loop(0, count, lambda index, carry: (body(index), carry)[1], 0)


def kernel(
    rows,
    cols,
    x_hbm,
    gain_hbm,
    bias_hbm,
    wl_hbm,
    bl_hbm,
    wr_hbm,
    br_hbm,
    w_hbm,
    bf_hbm,
    out,
    x_v,
    gain,
    bias,
    wlr,
    blr,
    w_v,
    bf,
    pl_v,
    pr_v,
    l_all,
    r_all,
    r_own,
    rt_v,
    wf_v,
    we_v,
    rolled_v,
    a_v,
    x_sem,
    in_sem,
    l_send,
    l_recv,
    r_send,
    r_recv,
):
    seqs, res, channels = x_v.shape
    hidden = wlr.shape[0] // 2
    groups = LANES // hidden
    tiles = res // groups
    ratio = rows // cols
    total = seqs * cols
    part = res // 2
    wide_half = res * hidden // 2
    copies_at = lax.axis_index("copies")
    row = lax.axis_index("row")
    col = lax.axis_index("col")
    target = row // ratio
    stays = col == target
    own = pl.ds(pl.multiple_of(col * seqs, seqs), seqs)

    barrier = pltpu.get_barrier_semaphore()

    def greet_left(step):
        peer = lax.rem(col + 1 + step, cols)
        pl.semaphore_signal(barrier, 1, device_id=(copies_at, row, peer), device_id_type=MESH)

    each(cols - 1, greet_left)

    def greet_right(step):
        source_row = col * ratio + step // cols
        source_col = lax.rem(step, cols)

        @pl.when(jnp.logical_not((source_row == row) & (source_col == col)))
        def _():
            pl.semaphore_signal(
                barrier, 1, device_id=(copies_at, source_row, source_col), device_id_type=MESH
            )

    each(ratio * cols, greet_right)

    loads = [
        pltpu.make_async_copy(source, place, in_sem.at[index])
        for index, (source, place) in enumerate(
            [
                (wl_hbm, wlr.at[0:hidden]),
                (wr_hbm, wlr.at[hidden : 2 * hidden]),
                (gain_hbm, gain),
                (bias_hbm, bias),
                (bl_hbm, blr.at[0:1]),
                (br_hbm, blr.at[1:2]),
                (w_hbm, w_v),
                (bf_hbm, bf),
            ]
        )
    ]
    x_part = seqs // X_PARTS
    x_loads = [
        pltpu.make_async_copy(
            x_hbm.at[piece_of * x_part : (piece_of + 1) * x_part],
            x_v.at[piece_of * x_part : (piece_of + 1) * x_part],
            x_sem.at[piece_of],
        )
        for piece_of in range(X_PARTS)
    ]
    for load in x_loads + loads[:6]:
        load.start()

    block = lax.broadcasted_iota(jnp.int32, (seqs, LANES), 1) // hidden

    for load in loads[:6]:
        load.wait()
    left_w, right_w = wlr[:hidden, :], wlr[hidden:, :]
    w8 = jnp.concatenate([left_w] * groups + [right_w] * groups, axis=0)
    bl4 = jnp.concatenate([blr[0:1, :]] * groups, axis=1)
    br4 = jnp.concatenate([blr[1:2, :]] * groups, axis=1)
    for piece_of in range(X_PARTS):
        x_loads[piece_of].wait()
        if piece_of == X_PARTS - 1:
            loads[6].start()
            loads[7].start()
        x = x_v[piece_of * x_part : (piece_of + 1) * x_part].astype(F32).reshape(x_part * res, channels)
        center = jnp.mean(x, axis=-1, keepdims=True)
        moved = x - center
        spread = jnp.mean(moved * moved, axis=-1, keepdims=True)
        normed = (moved * lax.rsqrt(spread + 1e-05) * gain[...] + bias[...]).astype(BF16)
        projected = lax.dot_general(normed, w8, (((1,), (1,)), ((), ())), preferred_element_type=F32)
        at = slice(piece_of * x_part * res, (piece_of + 1) * x_part * res)
        pl_v[at, :] = projected[:, :LANES]
        pr_v[at, :] = projected[:, LANES:]

    def spread_out(source, shift, tile):
        value = source[pl.ds(tile * groups, seqs, stride=res), :]
        for g in range(1, groups):
            value = jnp.where(block == g, source[pl.ds(tile * groups + g, seqs, stride=res), :], value)
        return (value + shift).astype(BF16)

    for tile in range(tiles):
        r_own[:, tile * LANES : (tile + 1) * LANES] = spread_out(pr_v, br4, tile)

    @pl.when(stays)
    def _():
        r_all[lax.rem(row, ratio), own, :] = r_own[...]

    for tile in range(tiles):
        l_all[own, tile * LANES : (tile + 1) * LANES] = spread_out(pl_v, bl4, tile)

    pl.semaphore_wait(barrier, cols - 1 + rows - stays.astype(jnp.int32))

    def right_copy(step, half):
        lanes = slice(half * wide_half, (half + 1) * wide_half)
        return pltpu.make_async_remote_copy(
            src_ref=r_own.at[:, lanes],
            dst_ref=r_all.at[lax.rem(row, ratio), own, lanes],
            send_sem=r_send.at[half, step],
            recv_sem=r_recv.at[half, lax.rem(row, ratio), col],
            device_id=(copies_at, lax.rem(row + 1 + step, rows), target),
            device_id_type=MESH,
        )

    for half in range(2):
        each(rows - 1, lambda step: right_copy(step, half).start())

        @pl.when(jnp.logical_not(stays))
        def _():
            right_copy(rows - 1, half).start()

    def left_copy(step):
        return pltpu.make_async_remote_copy(
            src_ref=l_all.at[own],
            dst_ref=l_all.at[own],
            send_sem=l_send.at[step],
            recv_sem=l_recv.at[col],
            device_id=(copies_at, row, lax.rem(col + 1 + step, cols)),
            device_id_type=MESH,
        )

    each(cols - 1, lambda step: left_copy(step).start())

    loads[6].wait()
    loads[7].wait()
    wf_v[...] = w_v[...].astype(F32)
    for e in range(hidden):
        we_v[e * hidden : (e + 1) * hidden, :] = wf_v[pl.ds(e, hidden, stride=hidden), :].astype(BF16)

    def left_wait(step):
        peer = lax.rem(col + 1 + step, cols)
        rows_of = pl.ds(pl.multiple_of(peer * seqs, seqs), seqs)
        pltpu.make_async_remote_copy(
            src_ref=l_all.at[rows_of],
            dst_ref=l_all.at[rows_of],
            send_sem=l_send.at[step],
            recv_sem=l_recv.at[peer],
            device_id=(copies_at, row, peer),
            device_id_type=MESH,
        ).wait_recv()

    lane_block = lax.rem(lax.broadcasted_iota(jnp.int32, (total, 2 * LANES), 1) // hidden, groups)

    each(cols - 1, left_wait)
    for tile in range(tiles):
        lanes = slice(tile * LANES, (tile + 1) * LANES)
        piece = l_all[:, lanes]
        rolled_v[0, :, lanes] = piece
        for low_e in range(1, groups):
            rolled_v[low_e, :, lanes] = pltpu.roll(piece.astype(F32), low_e * hidden, 1).astype(BF16)

    def columns(index, half):
        lanes_half = slice(half * wide_half, (half + 1) * wide_half)

        def right_wait(peer):
            rows_of = pl.ds(peer * seqs, seqs)

            @pl.when(jnp.logical_not((col * ratio + index == row) & (col == peer)))
            def _():
                pltpu.make_async_remote_copy(
                    src_ref=r_own.at[:, lanes_half],
                    dst_ref=r_all.at[index, rows_of, lanes_half],
                    send_sem=r_send.at[half, 0],
                    recv_sem=r_recv.at[half, index, peer],
                    device_id=(copies_at, row, col),
                    device_id_type=MESH,
                ).wait_recv()

        for peer in range(cols):
            right_wait(peer)
        for tile in range(half * tiles // 2, (half + 1) * tiles // 2):
            piece = r_all[index, :, tile * LANES : (tile + 1) * LANES].astype(F32)
            rt_v[tile * LANES : (tile + 1) * LANES, :total] = piece.T
        highs = hidden // groups
        lhs = jnp.concatenate(
            [
                jnp.concatenate(
                    [
                        rt_v[pl.ds(half * wide_half + high * groups + low_e, part, stride=hidden), :][:, :total]
                        for low_e in range(groups)
                    ],
                    axis=1,
                ).astype(BF16)
                for high in range(highs)
            ],
            axis=0,
        )
        for low_i in range(groups):
            for pair in range(tiles // 2):
                lanes = slice(2 * pair * LANES, 2 * (pair + 1) * LANES)
                rhs = jnp.concatenate(
                    [
                        jnp.where(lane_block == (low_e + low_i) % groups, rolled_v[low_e, :, lanes], 0)
                        for low_e in range(groups)
                    ],
                    axis=0,
                )
                outer = jnp.dot(lhs, rhs, preferred_element_type=F32).astype(BF16)
                for t in range(2):
                    tile = 2 * pair + t
                    for high in range(highs):
                        a_v[low_i, tile * part : (tile + 1) * part, high * LANES : (high + 1) * LANES] = outer[
                            high * part : (high + 1) * part, t * LANES : (t + 1) * LANES
                        ]
        for low_i in range(groups):
            weights = jnp.concatenate(
                [
                    we_v[e * hidden : (e + 1) * hidden, :]
                    for high in range(hidden // groups)
                    for e in [high * groups + (b - low_i) % groups for b in range(groups)]
                ],
                axis=0,
            )
            result = jnp.dot(a_v[low_i], weights, preferred_element_type=F32)
            result = (result * (1.0 / total) + bf[...]).astype(BF16)
            for tile in range(tiles):
                at = pl.ds(pl.multiple_of(index * res + half * part, part), part)
                out[tile * groups + low_i, at, :] = result[tile * part : (tile + 1) * part, :]

    for half in range(2):
        each(ratio, lambda index: columns(index, half))

    for half in range(2):
        each(rows - 1, lambda step: right_copy(step, half).wait_send())

        @pl.when(jnp.logical_not(stays))
        def _():
            right_copy(rows - 1, half).wait_send()

    each(cols - 1, lambda step: left_copy(step).wait_send())


def solution(mesh):
    rows, cols = mesh.shape["row"], mesh.shape["col"]

    def on_device(x, gain, bias, wl, bl, wr, br, w, bf):
        seqs, res, channels = x.shape
        hidden = wl.shape[1]
        outs = w.shape[1]
        ratio = rows // cols
        total = seqs * cols
        wide = res * hidden
        vmem = pl.BlockSpec(memory_space=pltpu.VMEM)
        hbm = pl.BlockSpec(memory_space=pltpu.HBM)
        groups = LANES // hidden
        return pl.pallas_call(
            functools.partial(kernel, rows, cols),
            out_shape=pltpu.VMEM((res, ratio * res, outs), BF16),
            in_specs=[hbm] * 9,
            out_specs=vmem,
            scratch_shapes=[
                pltpu.VMEM((seqs, res, channels), BF16),
                pltpu.VMEM((1, channels), F32),
                pltpu.VMEM((1, channels), F32),
                pltpu.VMEM((2 * hidden, channels), BF16),
                pltpu.VMEM((2, hidden), F32),
                pltpu.VMEM(w.shape, BF16),
                pltpu.VMEM((1, outs), F32),
                pltpu.VMEM((seqs * res, LANES), F32),
                pltpu.VMEM((seqs * res, LANES), F32),
                pltpu.VMEM((total, wide), BF16),
                pltpu.VMEM((ratio, total, wide), BF16),
                pltpu.VMEM((seqs, wide), BF16),
                pltpu.VMEM((wide, LANES), F32),
                pltpu.VMEM(w.shape, F32),
                pltpu.VMEM(w.shape, BF16),
                pltpu.VMEM((groups, total, wide), BF16),
                pltpu.VMEM((groups, wide // groups // 2, hidden * hidden), BF16),
                pltpu.SemaphoreType.DMA((X_PARTS,)),
                pltpu.SemaphoreType.DMA((8,)),
                pltpu.SemaphoreType.DMA((cols - 1,)),
                pltpu.SemaphoreType.DMA((cols,)),
                pltpu.SemaphoreType.DMA((2, rows)),
                pltpu.SemaphoreType.DMA((2, ratio, cols)),
            ],
            compiler_params=pltpu.CompilerParams(
                collective_id=0, has_side_effects=True, vmem_limit_bytes=48 * 1024 * 1024
            ),
        )(*[pltpu.with_memory_space_constraint(v, pltpu.HBM) for v in (x, gain[None], bias[None], wl.T, bl[None], wr.T, br[None], w, bf[None])])

    placed = (P(("copies", "col"), "row", None), P(), P(), P(), P(), P(), P(), P(), P())
    return jax.shard_map(
        on_device,
        mesh=mesh,
        in_specs=placed,
        out_specs=P(("copies", "row"), "col", None),
        check_vma=False,
    )
```
